32 devices in a mesh: groups: 1, gx: 4 (over z), gy: 4 (over y, x), gz: 2 (over core).
Axes of the slice: x: 2, y: 2, z: 4, core: 2. Of those that a mesh axis runs over, the one named last changes fastest.
Arguments:
- modes: float32 [3, 16, 32, 8, 128], P('groups', 'gx', 'gy', 'gz'), may hold values from -6 to 6
- cell_weight: float32 [16, 32, 8], P('gx', 'gy', 'gz'), may hold values from 0.25 to 4
- pair_owner: int32 [32], replicated, may hold values from 0 to 31, each once
Outputs:
- convective: float32 [64, 8256], P('groups', ('gx', 'gy', 'gz'))
The draws below stay inside these ranges and needn't reach their ends.
All inputs are finite; a program needn't handle non-finite values.
Results may differ from the reference program's by a relative error of at most 0.000098.
Values sent between devices are 32-bit elements; how exact they have to be, the bound alone decides.
A program may use at most 64 MiB of HBM per device.

```python
import math
import jax
import jax.numpy as jnp
import numpy as np
from jax import lax

MODES = 128
TEST = 64
NX = 16
NY = 32
NZ = 8
NOWN = 32
PAIRS = 8256
PBLK = 258
PAIRS_PAD = 8256


def levels(own_key, shape, shards, least, largest):
    def one(dim, parts):
        heights = jax.random.uniform(jax.random.fold_in(jax.random.fold_in(own_key, 6), dim), (parts,), jnp.float32, least / len(shards), largest / len(shards))
        return jnp.repeat(jnp.exp(heights), shape[dim] // parts).reshape((-1,) + (1,) * (len(shape) - dim - 1))

    factor_of = one(*shards[0])
    for cut in shards[1:]:
        factor_of = factor_of * one(*cut)
    return factor_of


def bell_draw(stream_key, shape, deviation, reach, shards=(), kind=jnp.bfloat16):
    values = deviation * jax.random.normal(stream_key, shape, jnp.float32)
    if shards:
        values = values * levels(stream_key, shape, shards, -0.22, 0.18)
    return jnp.clip(values, -reach, reach).astype(kind)


def setup_inputs(seed: int = 0, part: int = 0) -> dict:
    splits = jax.random.split(jax.random.key(seed), 4)
    part_splits = jax.random.split(jax.random.fold_in(splits[3], part), 4)
    return {
        "modes": bell_draw(part_splits[0], (3, NX, NY, NZ, MODES), 1.0, 6.0, ((1, 4), (2, 4), (3, 2)), jnp.float32),
        "cell_weight": jnp.clip(jnp.exp(math.log(4.0) - 2.7725887 * jax.random.uniform(splits[1], (NX, NY, NZ), jnp.float32) ** levels(splits[1], (NX, NY, NZ), ((0, 4), (1, 4), (2, 2)), -0.2, 0.2)), 0.25, 4.0),
        "pair_owner": jax.random.permutation(splits[2], NOWN).astype(jnp.int32),
    }


def gradients(padded):
    step_x = (padded[:, 2:, 1:-1, 1:-1] - padded[:, :-2, 1:-1, 1:-1]) * 0.5
    step_y = (padded[:, 1:-1, 2:, 1:-1] - padded[:, 1:-1, :-2, 1:-1]) * 0.5
    step_z = (padded[:, 1:-1, 1:-1, 2:] - padded[:, 1:-1, 1:-1, :-2]) * 0.5
    return jnp.stack([step_x, step_y, step_z], axis=1)

def assemble(mode_flat, grad_flat, weight_flat, test_count, block_size):
    weighted = mode_flat[:, :, :test_count] * weight_flat[None, :, None]
    cells = weighted.shape[1]
    blocks = weighted.reshape(3, cells, test_count // block_size, block_size).transpose(2, 0, 1, 3)

    def one_block(chosen):
        zeta = jnp.einsum('axi,abxk->ibxk', chosen, grad_flat, precision=lax.Precision.HIGHEST)
        return jnp.einsum('ibxk,bxj->ijk', zeta, mode_flat, precision=lax.Precision.HIGHEST)
    result = lax.map(one_block, blocks)
    width = mode_flat.shape[2]
    return result.reshape(test_count, width, width)

def reference(modes, cell_weight, pair_owner):
    wrapped = jnp.pad(modes, ((0, 0), (1, 1), (1, 1), (0, 0), (0, 0)), mode='wrap')
    padded = jnp.pad(wrapped, ((0, 0), (0, 0), (0, 0), (1, 1), (0, 0)))
    grads = gradients(padded)
    mode_flat = modes.reshape(3, -1, MODES)
    grad_flat = grads.reshape(3, 3, -1, MODES)
    weight_flat = cell_weight.reshape(-1)
    scale = 1.0 / jnp.sqrt(jnp.float32(3.0 * NX * NY * NZ))
    tensor = assemble(mode_flat, grad_flat, weight_flat, TEST, 1) * scale
    upper_j, upper_k = np.triu_indices(MODES)
    table_j = jnp.asarray(upper_j.astype(np.int32))
    table_k = jnp.asarray(upper_k.astype(np.int32))
    slots = jnp.arange(PAIRS_PAD, dtype=jnp.int32)
    owner_slot = slots // PBLK
    within = slots % PBLK
    pair_index = jnp.take(pair_owner, owner_slot) * PBLK + within
    valid = pair_index < PAIRS
    clipped = jnp.minimum(pair_index, PAIRS - 1)
    index_j = jnp.take(table_j, clipped)
    index_k = jnp.take(table_k, clipped)
    flattened = tensor.reshape(TEST, MODES * MODES)
    summed = jnp.take(flattened, index_j * MODES + index_k, axis=1) + jnp.take(flattened, index_k * MODES + index_j, axis=1)
    return jnp.where(valid[None, :], summed, jnp.float32(0.0))
```

```python
import functools
import math
import jax
import jax.numpy as jnp
from jax import lax
from jax.experimental import pallas as pl
from jax.experimental.pallas import tpu as pltpu
from jax.sharding import PartitionSpec as P

TEST = 64
LANES = 128
CHUNK = 688


def halo(value, axis, dim, periodic):
    peers, length = lax.axis_size(axis), value.shape[dim]
    up = [(i, (i + 1) % peers) for i in range(peers if periodic else peers - 1)]
    down = [(j, i) for i, j in up]
    last = lax.slice_in_dim(value, length - 1, length, axis=dim)
    leading = lax.slice_in_dim(value, 0, 1, axis=dim)
    return lax.ppermute(last, axis, up), lax.ppermute(leading, axis, down)


def gradient_tables(nx, ny, nz, m_ref, xb, xa, yb, ya, zb, za, mt, gt, ext, eyt, ezt):
    cells = nx * ny * nz
    plane = ny * nz
    width = m_ref.shape[-1]
    for a in range(3):
        m = m_ref[a]
        mt[a, pl.ds(0, width), :] = m.T
        mt[a, pl.ds(width, 8), :] = jnp.zeros((8, cells), jnp.float32)
        ext[pl.ds(0, plane), :] = xb[a]
        ext[pl.ds(plane, cells), :] = m
        ext[pl.ds(plane + cells, plane), :] = xa[a]
        step = (ext[pl.ds(2 * plane, cells), :] - ext[pl.ds(0, cells), :]) * 0.5
        gt[3 * a, pl.ds(0, width), :] = step.T
        for x in range(nx):
            eyt[x, pl.ds(0, nz), :] = yb[a, pl.ds(x * nz, nz), :]
            eyt[x, pl.ds(nz, plane), :] = m[x * plane:(x + 1) * plane]
            eyt[x, pl.ds(nz + plane, nz), :] = ya[a, pl.ds(x * nz, nz), :]
        step = (eyt[:, pl.ds(2 * nz, plane), :] - eyt[:, pl.ds(0, plane), :]) * 0.5
        gt[3 * a + 1, pl.ds(0, width), :] = step.reshape(cells, width).T
        ezt[0, pl.ds(8, cells), :] = m
        ezt[1, pl.ds(0, cells), :] = ezt[0, pl.ds(9, cells), :]
        ezt[0, pl.ds(0, cells), :] = ezt[0, pl.ds(7, cells), :]
        ezt[0, pl.ds(0, nx * ny, stride=nz), :] = zb[a]
        ezt[1, pl.ds(nz - 1, nx * ny, stride=nz), :] = za[a]
        step = (ezt[1, pl.ds(0, cells), :] - ezt[0, pl.ds(0, cells), :]) * 0.5
        gt[3 * a + 2, pl.ds(0, width), :] = step.T
        for b in range(3):
            gt[3 * a + b, pl.ds(width, 8), :] = jnp.zeros((8, cells), jnp.float32)


def pair_products(width, mt, gt, hbuf):
    for group in range(width // 8):
        tiles = width // 8 - group

        @pl.loop(group * 8, group * 8 + 8)
        def _(j):
            start = j * width - (j * (j - 1)) // 2
            mj = [mt[b, pl.ds(j, 1), :] for b in range(3)]
            gj = [gt[c, pl.ds(j, 1), :] for c in range(9)]
            for t in range(tiles):
                mk = [mt[b, pl.ds(j + 8 * t, 8), :] for b in range(3)]
                for a in range(3):
                    terms = [
                        mj[b] * gt[3 * a + b, pl.ds(j + 8 * t, 8), :] + gj[3 * a + b] * mk[b]
                        for b in range(3)
                    ]
                    hbuf[a, pl.ds(start + 8 * t, 8), :] = terms[0] + terms[1] + terms[2]


def split(value):
    high = value.astype(jnp.bfloat16)
    return high, (value - high.astype(jnp.float32)).astype(jnp.bfloat16)


def local_kernel(nx, ny, nz, block, half, rows, slots, scale, position, owner, m_ref, cw, xb, xa, yb, ya, zb, za,
                 out, mt, gt, hbuf, sbuf, rhs, ext, eyt, ezt):
    width = m_ref.shape[-1]
    pairs = width * (width + 1) // 2
    cells = nx * ny * nz
    gradient_tables(nx, ny, nz, m_ref, xb, xa, yb, ya, zb, za, mt, gt, ext, eyt, ezt)
    weight = cw[...] * scale
    for a in range(3):
        high, low = split(m_ref[a, :, pl.ds(0, TEST)] * weight)
        rhs[pl.ds(a * cells, cells), :] = jnp.concatenate([high, low], axis=1)
        rhs[pl.ds((3 + a) * cells, cells), :] = jnp.concatenate([high, jnp.zeros_like(low)], axis=1)
    pair_products(width, mt, gt, hbuf)

    @pl.loop(0, pairs // CHUNK)
    def _(c):
        here = pl.ds(pl.multiple_of(c * CHUNK, 16), CHUNK)
        parts = [split(hbuf[a, here, :]) for a in range(3)]
        left = jnp.concatenate([h for h, _ in parts] + [l for _, l in parts], axis=1)
        both = jnp.dot(left, rhs[...], preferred_element_type=jnp.float32)
        sbuf[here, :] = both + pltpu.roll(both, TEST, 1)

    spare = sbuf.shape[0] - pairs
    sbuf[pl.ds(pairs, spare), :] = jnp.zeros((spare, LANES), jnp.float32)
    first = lax.broadcasted_iota(jnp.int32, (rows, LANES), 1) < TEST

    @pl.loop(0, slots)
    def _(s):
        start = owner[s] * block
        low = sbuf[pl.ds(start, rows), :]
        high = sbuf[pl.ds(start + half, rows), :]
        out[position(s)] = jnp.where(first, low, high)


def local_tensor(modes, cell_weight, pair_owner, total_cells, block, position):
    _, nx, ny, nz, width = modes.shape
    cells = nx * ny * nz
    slots = pair_owner.shape[0]
    half = (block + 1) // 2
    rows = (half + 7) // 8 * 8
    xb, xa = halo(modes, "gx", 1, True)
    yb, ya = halo(modes, "gy", 2, True)
    zb, za = halo(modes, "gz", 3, False)
    flat = lambda v: v.reshape(3, -1, width)
    scale = 1.0 / math.sqrt(3.0 * total_cells)
    pairs = width * (width + 1) // 2
    sbuf_rows = (slots * block + half + rows + 7) // 8 * 8
    vmem = pl.BlockSpec(memory_space=pltpu.VMEM)
    return pl.pallas_call(
        functools.partial(local_kernel, nx, ny, nz, block, half, rows, slots, scale, position),
        out_shape=jax.ShapeDtypeStruct((slots, rows, LANES), jnp.float32),
        in_specs=[pl.BlockSpec(memory_space=pltpu.SMEM)] + [vmem] * 8,
        out_specs=vmem,
        scratch_shapes=[
            pltpu.VMEM((3, width + 8, cells), jnp.float32),
            pltpu.VMEM((9, width + 8, cells), jnp.float32),
            pltpu.VMEM((3, pairs + 8, cells), jnp.float32),
            pltpu.VMEM((sbuf_rows, LANES), jnp.float32),
            pltpu.VMEM((6 * cells, LANES), jnp.bfloat16),
            pltpu.VMEM((cells + 2 * ny * nz, width), jnp.float32),
            pltpu.VMEM((nx, ny * nz + 2 * nz, width), jnp.float32),
            pltpu.VMEM((2, cells + 16, width), jnp.float32),
        ],
        compiler_params=pltpu.CompilerParams(vmem_limit_bytes=48 * 1024 * 1024),
    )(pair_owner, flat(modes), cell_weight.reshape(cells, 1), flat(xb), flat(xa), flat(yb), flat(ya), flat(zb), flat(za))


def shards(modes, cell_weight, pair_owner):
    width = modes.shape[4]
    owners = lax.axis_size("gx") * lax.axis_size("gy") * lax.axis_size("gz")
    total_cells = modes.shape[1] * modes.shape[2] * modes.shape[3] * owners
    block = (width * (width + 1) // 2 + owners - 1) // owners
    half = (block + 1) // 2
    folded = local_tensor(modes, cell_weight, pair_owner, total_cells, block, lambda s: s)
    mine = lax.psum_scatter(folded, ("gx", "gy", "gz"), scatter_dimension=0, tiled=True)
    mine = lax.optimization_barrier(mine)[0, :half].reshape(half, 2, TEST).transpose(2, 1, 0)
    return mine.reshape(TEST, 2 * half)[:, :block]


def solution(mesh):
    placed = (P("groups", "gx", "gy", "gz", None), P("gx", "gy", "gz"), P())
    return jax.shard_map(
        shards,
        mesh=mesh,
        in_specs=placed,
        out_specs=P("groups", ("gx", "gy", "gz")),
        check_vma=False,
    )
```

```python
import functools
import math
import jax
import jax.numpy as jnp
from jax import lax
from jax.experimental import pallas as pl
from jax.experimental.pallas import tpu as pltpu
from jax.sharding import PartitionSpec as P

TEST = 64
LANES = 128
CHUNK = 688


def halo(value, axis, dim, periodic):
    peers, length = lax.axis_size(axis), value.shape[dim]
    up = [(i, (i + 1) % peers) for i in range(peers if periodic else peers - 1)]
    down = [(j, i) for i, j in up]
    last = lax.slice_in_dim(value, length - 1, length, axis=dim)
    leading = lax.slice_in_dim(value, 0, 1, axis=dim)
    return lax.ppermute(last, axis, up), lax.ppermute(leading, axis, down)


def gradient_tables(nx, ny, nz, m_ref, xb, xa, yb, ya, zb, za, mt, gt, ext, eyt, ezt):
    cells = nx * ny * nz
    plane = ny * nz
    width = m_ref.shape[-1]
    for a in range(3):
        m = m_ref[a]
        mt[a, pl.ds(0, width), :] = m.T
        mt[a, pl.ds(width, 8), :] = jnp.zeros((8, cells), jnp.float32)
        ext[pl.ds(0, plane), :] = xb[a]
        ext[pl.ds(plane, cells), :] = m
        ext[pl.ds(plane + cells, plane), :] = xa[a]
        step = (ext[pl.ds(2 * plane, cells), :] - ext[pl.ds(0, cells), :]) * 0.5
        gt[3 * a, pl.ds(0, width), :] = step.T
        for x in range(nx):
            eyt[x, pl.ds(0, nz), :] = yb[a, pl.ds(x * nz, nz), :]
            eyt[x, pl.ds(nz, plane), :] = m[x * plane:(x + 1) * plane]
            eyt[x, pl.ds(nz + plane, nz), :] = ya[a, pl.ds(x * nz, nz), :]
        step = (eyt[:, pl.ds(2 * nz, plane), :] - eyt[:, pl.ds(0, plane), :]) * 0.5
        gt[3 * a + 1, pl.ds(0, width), :] = step.reshape(cells, width).T
        ezt[0, pl.ds(8, cells), :] = m
        ezt[1, pl.ds(0, cells), :] = ezt[0, pl.ds(9, cells), :]
        ezt[0, pl.ds(0, cells), :] = ezt[0, pl.ds(7, cells), :]
        ezt[0, pl.ds(0, nx * ny, stride=nz), :] = zb[a]
        ezt[1, pl.ds(nz - 1, nx * ny, stride=nz), :] = za[a]
        step = (ezt[1, pl.ds(0, cells), :] - ezt[0, pl.ds(0, cells), :]) * 0.5
        gt[3 * a + 2, pl.ds(0, width), :] = step.T
        for b in range(3):
            gt[3 * a + b, pl.ds(width, 8), :] = jnp.zeros((8, cells), jnp.float32)


def pair_products(width, mt, gt, hbuf):
    for group in range(width // 8):
        tiles = width // 8 - group

        @pl.loop(group * 8, group * 8 + 8)
        def _(j):
            start = j * width - (j * (j - 1)) // 2
            mj = [mt[b, pl.ds(j, 1), :] for b in range(3)]
            gj = [gt[c, pl.ds(j, 1), :] for c in range(9)]
            for t in range(tiles):
                mk = [mt[b, pl.ds(j + 8 * t, 8), :] for b in range(3)]
                for a in range(3):
                    terms = [
                        mj[b] * gt[3 * a + b, pl.ds(j + 8 * t, 8), :] + gj[3 * a + b] * mk[b]
                        for b in range(3)
                    ]
                    hbuf[a, pl.ds(start + 8 * t, 8), :] = terms[0] + terms[1] + terms[2]


def split(value):
    high = value.astype(jnp.bfloat16)
    return high, (value - high.astype(jnp.float32)).astype(jnp.bfloat16)


def local_kernel(nx, ny, nz, block, half, rows, slots, scale, position, owner, m_ref, cw, xb, xa, yb, ya, zb, za,
                 out, mt, gt, hbuf, sbuf, rhs, ext, eyt, ezt):
    width = m_ref.shape[-1]
    pairs = width * (width + 1) // 2
    cells = nx * ny * nz
    gradient_tables(nx, ny, nz, m_ref, xb, xa, yb, ya, zb, za, mt, gt, ext, eyt, ezt)
    weight = cw[...] * scale
    for a in range(3):
        high, low = split(m_ref[a, :, pl.ds(0, TEST)] * weight)
        rhs[pl.ds(a * cells, cells), :] = jnp.concatenate([high, low], axis=1)
        rhs[pl.ds((3 + a) * cells, cells), :] = jnp.concatenate([high, jnp.zeros_like(low)], axis=1)
    pair_products(width, mt, gt, hbuf)

    @pl.loop(0, pairs // CHUNK)
    def _(c):
        here = pl.ds(pl.multiple_of(c * CHUNK, 16), CHUNK)
        parts = [split(hbuf[a, here, :]) for a in range(3)]
        left = jnp.concatenate([h for h, _ in parts] + [l for _, l in parts], axis=1)
        both = jnp.dot(left, rhs[...], preferred_element_type=jnp.float32)
        sbuf[here, :] = both + pltpu.roll(both, TEST, 1)

    spare = sbuf.shape[0] - pairs
    sbuf[pl.ds(pairs, spare), :] = jnp.zeros((spare, LANES), jnp.float32)
    first = lax.broadcasted_iota(jnp.int32, (rows, LANES), 1) < TEST

    @pl.loop(0, slots)
    def _(s):
        start = owner[s] * block
        low = sbuf[pl.ds(start, rows), :]
        high = sbuf[pl.ds(start + half, rows), :]
        out[position(s)] = jnp.where(first, low, high)


def local_tensor(modes, cell_weight, pair_owner, total_cells, block, position):
    _, nx, ny, nz, width = modes.shape
    cells = nx * ny * nz
    slots = pair_owner.shape[0]
    half = (block + 1) // 2
    rows = (half + 7) // 8 * 8
    xb, xa = halo(modes, "gx", 1, True)
    yb, ya = halo(modes, "gy", 2, True)
    zb, za = halo(modes, "gz", 3, False)
    flat = lambda v: v.reshape(3, -1, width)
    scale = 1.0 / math.sqrt(3.0 * total_cells)
    pairs = width * (width + 1) // 2
    sbuf_rows = (slots * block + half + rows + 7) // 8 * 8
    vmem = pl.BlockSpec(memory_space=pltpu.VMEM)
    return pl.pallas_call(
        functools.partial(local_kernel, nx, ny, nz, block, half, rows, slots, scale, position),
        out_shape=jax.ShapeDtypeStruct((slots, rows, LANES), jnp.float32),
        in_specs=[pl.BlockSpec(memory_space=pltpu.SMEM)] + [vmem] * 8,
        out_specs=vmem,
        scratch_shapes=[
            pltpu.VMEM((3, width + 8, cells), jnp.float32),
            pltpu.VMEM((9, width + 8, cells), jnp.float32),
            pltpu.VMEM((3, pairs + 8, cells), jnp.float32),
            pltpu.VMEM((sbuf_rows, LANES), jnp.float32),
            pltpu.VMEM((6 * cells, LANES), jnp.bfloat16),
            pltpu.VMEM((cells + 2 * ny * nz, width), jnp.float32),
            pltpu.VMEM((nx, ny * nz + 2 * nz, width), jnp.float32),
            pltpu.VMEM((2, cells + 16, width), jnp.float32),
        ],
        compiler_params=pltpu.CompilerParams(vmem_limit_bytes=48 * 1024 * 1024),
    )(pair_owner, flat(modes), cell_weight.reshape(cells, 1), flat(xb), flat(xa), flat(yb), flat(ya), flat(zb), flat(za))


def bit_of(value, bit):
    return lax.rem(value // (1 << bit), 2)


def owned_kernel(nx, ny, nz, block, part, out, acc, from_core, from_gy, from_gx, core_send, core_recv, gy_send, gy_recv,
                 gx_send, gx_recv):
    cx, cy, cz = (lax.axis_index(name) for name in ("gx", "gy", "gz"))
    bits = ny.bit_length() - 1
    other = 1 - cz
    mine = [bit_of(cy, b) for b in range(bits)]

    def position(mask):
        return sum((1 - mine[b] if mask >> b & 1 else mine[b]) * (1 << b) for b in range(bits))

    barrier = pltpu.get_barrier_semaphore()
    partners = [{"gz": other}] + [{"gy": position(1 << b)} for b in range(bits)]
    partners += [{"gx": lax.rem(cx + d, nx)} for d in range(1, nx)]
    for partner in partners:
        pl.semaphore_signal(barrier, inc=1, device_id=partner, device_id_type=pl.DeviceIdType.MESH)
    pl.semaphore_wait(barrier, len(partners))

    def remote(src, dst, send, recv, device):
        return pltpu.make_async_remote_copy(
            src_ref=src, dst_ref=dst, send_sem=send, recv_sem=recv, device_id=device,
            device_id_type=pl.DeviceIdType.MESH,
        )

    orders = [list(range(bits)), list(reversed(range(bits)))]

    def rank(h, mask):
        return sum((mask >> b & 1) << (bits - 1 - k) for k, b in enumerate(orders[h]))

    sequence = [sorted(range(ny), key=lambda m: -rank(h, m)) for h in range(2)]
    pending = []
    first = {}
    for at in range(ny):
        for h in range(2):
            m = sequence[h][at]
            copy = remote(part.at[h, other, position(m)], from_core.at[h, m], core_send.at[h, m], core_recv.at[h, m],
                          {"gz": other})
            copy.start()
            first[h, m] = copy
            pending.append(copy)

    def step_of(h, mask):
        return next(k for k, b in enumerate(orders[h]) if mask >> b & 1)

    hops = {}

    def send(h, m):
        b = orders[h][step_of(h, m)]
        copy = remote(acc.at[h, m], from_gy.at[h, m], gy_send.at[h, m], gy_recv.at[h, m], {"gy": position(1 << b)})
        copy.start()
        hops[h, m] = copy
        pending.append(copy)

    for at in range(ny):
        for h in range(2):
            m = sequence[h][at]
            first[h, m].wait_recv()
            acc[h, m] = part[h, cz, position(m)] + from_core[h, m]
            if m and step_of(h, m) == 0:
                send(h, m)
    for k in range(bits):
        for at in range(ny):
            for h in range(2):
                m = sequence[h][at]
                if m and step_of(h, m) == k:
                    hops[h, m].wait_recv()
                    left = m ^ (1 << orders[h][k])
                    acc[h, left] = acc[h, left] + from_gy[h, m]
                    if left and step_of(h, left) == k + 1:
                        send(h, left)
    lines = []
    for d in range(1, nx):
        to = lax.rem(cx + d, nx)
        copy = remote(acc.at[to // (nx // 2), 0, lax.rem(to, nx // 2)], from_gx.at[d - 1], gx_send.at[d - 1],
                      gx_recv.at[d - 1], {"gx": to})
        copy.start()
        lines.append(copy)
        pending.append(copy)
    total = acc[cx // (nx // 2), 0, lax.rem(cx, nx // 2)]
    for d in range(1, nx):
        lines[d - 1].wait_recv()
        total = total + from_gx[d - 1]
    half = (block + 1) // 2
    turned = total.T
    out[...] = jnp.concatenate([turned[:TEST, :half], turned[TEST:, :block - half]], axis=1)
    for copy in pending:
        copy.wait_send()


def owned_block(part, block):
    _, nz, ny, hx, rows, _ = part.shape
    nx = 2 * hx
    piece = (2, ny, hx, rows, LANES)
    vmem = pl.BlockSpec(memory_space=pltpu.VMEM)
    dma = pltpu.SemaphoreType.DMA
    return pl.pallas_call(
        functools.partial(owned_kernel, nx, ny, nz, block),
        out_shape=jax.ShapeDtypeStruct((TEST, block), jnp.float32),
        in_specs=[vmem],
        out_specs=vmem,
        scratch_shapes=[pltpu.VMEM(piece, jnp.float32)] * 3 + [pltpu.VMEM((nx - 1, rows, LANES), jnp.float32)]
        + [dma((2, ny))] * 4 + [dma((nx - 1,))] * 2,
        compiler_params=pltpu.CompilerParams(
            collective_id=0, has_side_effects=True, vmem_limit_bytes=48 * 1024 * 1024
        ),
    )(part)


def shards(modes, cell_weight, pair_owner):
    width = modes.shape[4]
    nx, ny, nz = (lax.axis_size(name) for name in ("gx", "gy", "gz"))
    owners = nx * ny * nz
    total_cells = modes.shape[1] * modes.shape[2] * modes.shape[3] * owners
    block = (width * (width + 1) // 2 + owners - 1) // owners
    hx = nx // 2

    def position(s):
        cx, cy, cz = s // (ny * nz), lax.rem(s // nz, ny), lax.rem(s, nz)
        return (((cx // hx) * nz + cz) * ny + cy) * hx + lax.rem(cx, hx)

    folded = local_tensor(modes, cell_weight, pair_owner, total_cells, block, position)
    return owned_block(folded.reshape(2, nz, ny, hx, *folded.shape[1:]), block)


def solution(mesh):
    placed = (P("groups", "gx", "gy", "gz", None), P("gx", "gy", "gz"), P())
    return jax.shard_map(
        shards,
        mesh=mesh,
        in_specs=placed,
        out_specs=P("groups", ("gx", "gy", "gz")),
        check_vma=False,
    )
```

```python
import functools
import math
import jax
import jax.numpy as jnp
from jax import lax
from jax.experimental import pallas as pl
from jax.experimental.pallas import tpu as pltpu
from jax.sharding import PartitionSpec as P

TEST = 64
LANES = 128
CHUNK = 688
STAGES = 4


def bounds(rows):
    tiles = rows // 8
    stages = min(STAGES, tiles)
    cuts = [8 * (tiles * c // stages) for c in range(stages + 1)]
    return [(a, b - a) for a, b in zip(cuts, cuts[1:])]


def transposed_gradients(lx, ly, lz, level, m_ref, faces, gt, ext, eyt, ezt):
    cells, plane, width = lx * ly * lz, ly * lz, m_ref.shape[-1]
    x_before, x_after, y_before, y_after, z_face = faces
    for a in range(3):
        m = m_ref[a].reshape(cells, width)
        ext[pl.ds(0, plane), :] = x_before[a, 0]
        ext[pl.ds(plane, cells), :] = m
        ext[pl.ds(plane + cells, plane), :] = x_after[a, 0]
        step = (ext[pl.ds(2 * plane, cells), :] - ext[pl.ds(0, cells), :]) * 0.5
        gt[3 * a, pl.ds(0, width), :] = step.T
        for x in range(lx):
            eyt[x, pl.ds(0, lz), :] = y_before[a, x, pl.ds(8 - lz, lz), :]
            eyt[x, pl.ds(lz, plane), :] = m_ref[a, x]
            eyt[x, pl.ds(lz + plane, lz), :] = y_after[a, x, pl.ds(0, lz), :]
        step = (eyt[:, pl.ds(2 * lz, plane), :] - eyt[:, pl.ds(0, plane), :]) * 0.5
        gt[3 * a + 1, pl.ds(0, width), :] = step.reshape(cells, width).T
        ezt[0, pl.ds(8, cells), :] = m
        ezt[1, pl.ds(0, cells), :] = ezt[0, pl.ds(9, cells), :]
        ezt[0, pl.ds(0, cells), :] = ezt[0, pl.ds(7, cells), :]
        ezt[0, pl.ds(0, lx * ly, stride=lz), :] = jnp.where(level == 1, z_face[a], 0.0)
        ezt[1, pl.ds(lz - 1, lx * ly, stride=lz), :] = jnp.where(level == 0, z_face[a], 0.0)
        step = (ezt[1, pl.ds(0, cells), :] - ezt[0, pl.ds(0, cells), :]) * 0.5
        gt[3 * a + 2, pl.ds(0, width), :] = step.T
        for b in range(3):
            gt[3 * a + b, pl.ds(width, 8), :] = jnp.zeros((8, cells), jnp.float32)


def pair_products(width, mt, gt, hbuf):
    for group in range(width // 8):
        tiles = width // 8 - group

        @pl.loop(group * 8, group * 8 + 8)
        def _(j):
            start = j * width - (j * (j - 1)) // 2
            mj = [mt[b, pl.ds(j, 1), :] for b in range(3)]
            gj = [gt[c, pl.ds(j, 1), :] for c in range(9)]
            for t in range(tiles):
                mk = [mt[b, pl.ds(j + 8 * t, 8), :] for b in range(3)]
                for a in range(3):
                    terms = [
                        mj[b] * gt[3 * a + b, pl.ds(j + 8 * t, 8), :] + gj[3 * a + b] * mk[b]
                        for b in range(3)
                    ]
                    hbuf[a, pl.ds(start + 8 * t, 8), :] = terms[0] + terms[1] + terms[2]


def split(value):
    high = value.astype(jnp.bfloat16)
    return high, (value - high.astype(jnp.float32)).astype(jnp.bfloat16)


def bit_of(value, bit):
    return lax.rem(value // (1 << bit), 2)


def convective_kernel(mesh_shape, local_shape, block, scale, owner, m_ref, cw, out,
                      x_before, x_after, y_before, y_after, z_face, z_out, mt, gt, hbuf, sbuf, rhs, ext, eyt, ezt,
                      part, acc, from_core, from_gy, from_gx, face_send, face_recv,
                      core_send, core_recv, gy_send, gy_recv, gx_send, gx_recv):
    nx, ny, nz = mesh_shape
    lx, ly, lz = local_shape
    cells, plane, width = lx * ly * lz, ly * lz, m_ref.shape[-1]
    pairs = width * (width + 1) // 2
    half = (block + 1) // 2
    hx = nx // 2
    parts = bounds(acc.shape[3])
    cx, cy, cz = (lax.axis_index(name) for name in ("gx", "gy", "gz"))
    other = 1 - cz
    bits = ny.bit_length() - 1
    mine = [bit_of(cy, b) for b in range(bits)]

    def position(mask):
        return sum((1 - mine[b] if mask >> b & 1 else mine[b]) * (1 << b) for b in range(bits))

    pending = []

    def remote(src, dst, send, recv, device):
        copy = pltpu.make_async_remote_copy(
            src_ref=src, dst_ref=dst, send_sem=send, recv_sem=recv, device_id=device,
            device_id_type=pl.DeviceIdType.MESH,
        )
        copy.start()
        pending.append(copy)
        return copy

    barrier = pltpu.get_barrier_semaphore()
    partners = [{"gz": other}] + [{"gy": lax.rem(cy + d, ny)} for d in range(1, ny)]
    partners += [{"gx": lax.rem(cx + d, nx)} for d in range(1, nx)]
    for partner in partners:
        pl.semaphore_signal(barrier, inc=1, device_id=partner, device_id_type=pl.DeviceIdType.MESH)
    for a in range(3):
        m = m_ref[a].reshape(cells, width)
        ezt[0, pl.ds(0, cells), :] = m
        top = ezt[0, pl.ds(lz - 1, lx * ly, stride=lz), :]
        bottom = ezt[0, pl.ds(0, lx * ly, stride=lz), :]
        z_out[a] = jnp.where(cz == 0, top, bottom)
    pl.semaphore_wait(barrier, len(partners))

    arrivals = [
        remote(m_ref.at[:, pl.ds(lx - 1, 1)], x_before, face_send.at[0], face_recv.at[0], {"gx": lax.rem(cx + 1, nx)}),
        remote(m_ref.at[:, pl.ds(0, 1)], x_after, face_send.at[1], face_recv.at[1], {"gx": lax.rem(cx + nx - 1, nx)}),
        remote(m_ref.at[:, :, pl.ds(plane - 8, 8)], y_before, face_send.at[2], face_recv.at[2],
               {"gy": lax.rem(cy + 1, ny)}),
        remote(m_ref.at[:, :, pl.ds(0, 8)], y_after, face_send.at[3], face_recv.at[3],
               {"gy": lax.rem(cy + ny - 1, ny)}),
        remote(z_out, z_face, face_send.at[4], face_recv.at[4], {"gz": other}),
    ]
    weight = cw[...] * scale
    for a in range(3):
        m = m_ref[a].reshape(cells, width)
        mt[a, pl.ds(0, width), :] = m.T
        mt[a, pl.ds(width, 8), :] = jnp.zeros((8, cells), jnp.float32)
        high, low = split(m[:, :TEST] * weight)
        rhs[pl.ds(a * cells, cells), :] = jnp.concatenate([high, low], axis=1)
        rhs[pl.ds((3 + a) * cells, cells), :] = jnp.concatenate([high, jnp.zeros_like(low)], axis=1)
    spare = sbuf.shape[0] - pairs
    sbuf[pl.ds(pairs, spare), :] = jnp.zeros((spare, LANES), jnp.float32)
    for copy in arrivals:
        copy.wait_recv()
    transposed_gradients(lx, ly, lz, cz, m_ref, (x_before, x_after, y_before, y_after, z_face), gt, ext, eyt, ezt)
    pair_products(width, mt, gt, hbuf)

    @pl.loop(0, pairs // CHUNK)
    def _(c):
        here = pl.ds(pl.multiple_of(c * CHUNK, 16), CHUNK)
        pieces = [split(hbuf[a, here, :]) for a in range(3)]
        left = jnp.concatenate([h for h, _ in pieces] + [l for _, l in pieces], axis=1)
        both = jnp.dot(left, rhs[...], preferred_element_type=jnp.float32)
        sbuf[here, :] = both + pltpu.roll(both, TEST, 1)

    def folded(h, mask, level, t, rows_from, count):
        slot = ((h * hx + t) * ny + position(mask)) * nz + level
        start = owner[slot] * block + rows_from
        first = lax.broadcasted_iota(jnp.int32, (count, LANES), 1) < TEST
        return jnp.where(first, sbuf[pl.ds(start, count), :], sbuf[pl.ds(start + half, count), :])

    orders = [list(range(bits)), list(reversed(range(bits)))]

    def rank(h, mask):
        return sum((mask >> b & 1) << (bits - 1 - k) for k, b in enumerate(orders[h]))

    def step_of(h, mask):
        return next(k for k, b in enumerate(orders[h]) if mask >> b & 1)

    sequence = [(h, m) for at in range(ny) for h, m in
                [(h, sorted(range(ny), key=lambda m: -rank(h, m))[at]) for h in range(2)]]
    first_hop, hops, lines = {}, {}, {}

    def send(c, h, m):
        b = orders[h][step_of(h, m)]
        rows = pl.ds(*parts[c])
        hops[c, h, m] = remote(acc.at[h, m, :, rows], from_gy.at[h, m, :, rows], gy_send.at[c, h, m],
                               gy_recv.at[c, h, m], {"gy": position(1 << b)})

    def across_cores(c):
        rows_from, count = parts[c]
        rows = pl.ds(rows_from, count)
        for h, m in sequence:
            @pl.loop(0, hx)
            def _(t):
                part[h, m, t, rows, :] = folded(h, m, other, t, rows_from, count)

            first_hop[c, h, m] = remote(part.at[h, m, :, rows], from_core.at[h, m, :, rows], core_send.at[c, h, m],
                                        core_recv.at[c, h, m], {"gz": other})

    def chip_sums(c):
        rows_from, count = parts[c]
        rows = pl.ds(rows_from, count)
        for h, m in sequence:
            first_hop[c, h, m].wait_recv()

            @pl.loop(0, hx)
            def _(t):
                acc[h, m, t, rows, :] = folded(h, m, cz, t, rows_from, count) + from_core[h, m, t, rows, :]

            if m and step_of(h, m) == 0:
                send(c, h, m)

    def across_gy(c, k):
        rows = pl.ds(*parts[c])
        for h, m in sequence:
            if m and step_of(h, m) == k:
                hops[c, h, m].wait_recv()
                left = m ^ (1 << orders[h][k])
                acc[h, left, :, rows, :] = acc[h, left, :, rows, :] + from_gy[h, m, :, rows, :]
                if left and step_of(h, left) == k + 1:
                    send(c, h, left)
        if k == bits - 1:
            for d in range(1, nx):
                to = lax.rem(cx + d, nx)
                lines[c, d] = remote(acc.at[to // hx, 0, lax.rem(to, hx), rows], from_gx.at[d - 1, rows],
                                     gx_send.at[c, d - 1], gx_recv.at[c, d - 1], {"gx": to})

    stages = [across_cores, chip_sums] + [functools.partial(across_gy, k=k) for k in range(bits)]
    for wave in range(len(parts) + len(stages) - 1):
        for k, stage in enumerate(stages):
            if 0 <= wave - k < len(parts):
                stage(wave - k)
    sums = []
    for c, (rows_from, count) in enumerate(parts):
        rows = pl.ds(rows_from, count)
        total = acc[cx // hx, 0, lax.rem(cx, hx), rows, :]
        for d in range(1, nx):
            lines[c, d].wait_recv()
            total = total + from_gx[d - 1, rows, :]
        sums.append(total)
    turned = jnp.concatenate(sums, axis=0).T
    out[...] = jnp.concatenate([turned[:TEST, :half], turned[TEST:, :block - half]], axis=1)
    for copy in pending:
        copy.wait_send()


def shards(modes, cell_weight, pair_owner):
    _, lx, ly, lz, width = modes.shape
    nx, ny, nz = (lax.axis_size(name) for name in ("gx", "gy", "gz"))
    slots = nx * ny * nz
    cells, plane = lx * ly * lz, ly * lz
    pairs = width * (width + 1) // 2
    block = (pairs + slots - 1) // slots
    half = (block + 1) // 2
    rows = (half + 7) // 8 * 8
    hx = nx // 2
    scale = 1.0 / math.sqrt(3.0 * cells * slots)
    sbuf_rows = (slots * block + half + rows + 7) // 8 * 8
    stages = len(bounds(rows))
    vmem = pl.BlockSpec(memory_space=pltpu.VMEM)
    dma = pltpu.SemaphoreType.DMA

    def buffer(*shape):
        return pltpu.VMEM(shape, jnp.float32)

    return pl.pallas_call(
        functools.partial(convective_kernel, (nx, ny, nz), (lx, ly, lz), block, scale),
        out_shape=jax.ShapeDtypeStruct((TEST, block), jnp.float32),
        in_specs=[pl.BlockSpec(memory_space=pltpu.SMEM), vmem, vmem],
        out_specs=vmem,
        scratch_shapes=[
            buffer(3, 1, plane, width), buffer(3, 1, plane, width),
            buffer(3, lx, 8, width), buffer(3, lx, 8, width),
            buffer(3, lx * ly, width), buffer(3, lx * ly, width),
            buffer(3, width + 8, cells), buffer(9, width + 8, cells),
            buffer(3, pairs + 8, cells), buffer(sbuf_rows, LANES),
            pltpu.VMEM((6 * cells, LANES), jnp.bfloat16),
            buffer(cells + 2 * plane, width), buffer(lx, plane + 2 * lz, width), buffer(2, cells + 16, width),
            buffer(2, ny, hx, rows, LANES), buffer(2, ny, hx, rows, LANES),
            buffer(2, ny, hx, rows, LANES), buffer(2, ny, hx, rows, LANES),
            buffer(nx - 1, rows, LANES),
            dma((5,)), dma((5,)),
        ] + [dma((stages, 2, ny))] * 4 + [dma((stages, nx - 1))] * 2,
        compiler_params=pltpu.CompilerParams(
            collective_id=0, has_side_effects=True, vmem_limit_bytes=48 * 1024 * 1024
        ),
    )(pair_owner, modes.reshape(3, lx, plane, width), cell_weight.reshape(cells, 1))


def solution(mesh):
    placed = (P("groups", "gx", "gy", "gz", None), P("gx", "gy", "gz"), P())
    return jax.shard_map(
        shards,
        mesh=mesh,
        in_specs=placed,
        out_specs=P("groups", ("gx", "gy", "gz")),
        check_vma=False,
    )
```

```python
import functools
import math
import jax
import jax.numpy as jnp
from jax import lax
from jax.experimental import pallas as pl
from jax.experimental.pallas import tpu as pltpu
from jax.sharding import PartitionSpec as P

TEST = 64
LANES = 128
STAGES = 4


def bounds(rows):
    tiles = rows // 8
    stages = min(STAGES, tiles)
    cuts = [8 * (tiles * c // stages) for c in range(stages + 1)]
    return [(a, b - a) for a, b in zip(cuts, cuts[1:])]


def transposed_gradients(lx, ly, lz, level, m_ref, faces, gt, ext, eyt, ezt):
    cells, plane, width = lx * ly * lz, ly * lz, m_ref.shape[-1]
    x_before, x_after, y_before, y_after, z_face = faces
    for a in range(3):
        m = m_ref[a].reshape(cells, width)
        ext[pl.ds(0, plane), :] = x_before[a, 0]
        ext[pl.ds(plane, cells), :] = m
        ext[pl.ds(plane + cells, plane), :] = x_after[a, 0]
        step = (ext[pl.ds(2 * plane, cells), :] - ext[pl.ds(0, cells), :]) * 0.5
        gt[3 * a, pl.ds(0, width), :] = step.T
        for x in range(lx):
            eyt[x, pl.ds(0, lz), :] = y_before[a, x, pl.ds(8 - lz, lz), :]
            eyt[x, pl.ds(lz, plane), :] = m_ref[a, x]
            eyt[x, pl.ds(lz + plane, lz), :] = y_after[a, x, pl.ds(0, lz), :]
        step = (eyt[:, pl.ds(2 * lz, plane), :] - eyt[:, pl.ds(0, plane), :]) * 0.5
        gt[3 * a + 1, pl.ds(0, width), :] = step.reshape(cells, width).T
        ezt[0, pl.ds(8, cells), :] = m
        ezt[1, pl.ds(0, cells), :] = ezt[0, pl.ds(9, cells), :]
        ezt[0, pl.ds(0, cells), :] = ezt[0, pl.ds(7, cells), :]
        ezt[0, pl.ds(0, lx * ly, stride=lz), :] = jnp.where(level == 1, z_face[a], 0.0)
        ezt[1, pl.ds(lz - 1, lx * ly, stride=lz), :] = jnp.where(level == 0, z_face[a], 0.0)
        step = (ezt[1, pl.ds(0, cells), :] - ezt[0, pl.ds(0, cells), :]) * 0.5
        gt[3 * a + 2, pl.ds(0, width), :] = step.T
        for b in range(3):
            gt[3 * a + b, pl.ds(width, 8), :] = jnp.zeros((8, cells), jnp.float32)


def pair_products(width, mt, gt, hbuf):
    for group in range(width // 8):
        tiles = width // 8 - group

        @pl.loop(group * 8, group * 8 + 8)
        def _(j):
            start = j * width - (j * (j - 1)) // 2
            mj = [mt[b, pl.ds(j, 1), :] for b in range(3)]
            gj = [gt[c, pl.ds(j, 1), :] for c in range(9)]
            for t in range(tiles):
                mk = [mt[b, pl.ds(j + 8 * t, 8), :] for b in range(3)]
                for a in range(3):
                    terms = [
                        mj[b] * gt[3 * a + b, pl.ds(j + 8 * t, 8), :] + gj[3 * a + b] * mk[b]
                        for b in range(3)
                    ]
                    hbuf[a, pl.ds(start + 8 * t, 8), :] = terms[0] + terms[1] + terms[2]


def split(value):
    high = value.astype(jnp.bfloat16)
    return high, (value - high.astype(jnp.float32)).astype(jnp.bfloat16)


def bit_of(value, bit):
    return lax.rem(value // (1 << bit), 2)


def convective_kernel(mesh_shape, local_shape, block, scale, owner, m_hbm, cw_hbm, out, m_ref, cw, load,
                      x_before, x_after, y_before, y_after, z_face, z_out, mt, gt, hbuf, lhs, rhs, wide, ext, eyt, ezt,
                      part, acc, from_core, from_gy, from_gx, face_send, face_recv,
                      core_send, core_recv, gy_send, gy_recv, gx_send, gx_recv):
    nx, ny, nz = mesh_shape
    lx, ly, lz = local_shape
    cells, plane, width = lx * ly * lz, ly * lz, m_ref.shape[-1]
    pairs = width * (width + 1) // 2
    half = (block + 1) // 2
    hx = nx // 2
    parts = bounds(acc.shape[3])
    cx, cy, cz = (lax.axis_index(name) for name in ("gx", "gy", "gz"))
    other = 1 - cz
    bits = ny.bit_length() - 1
    mine = [bit_of(cy, b) for b in range(bits)]

    def position(mask):
        return sum((1 - mine[b] if mask >> b & 1 else mine[b]) * (1 << b) for b in range(bits))

    pending = []

    def remote(src, dst, send, recv, device):
        copy = pltpu.make_async_remote_copy(
            src_ref=src, dst_ref=dst, send_sem=send, recv_sem=recv, device_id=device,
            device_id_type=pl.DeviceIdType.MESH,
        )
        copy.start()
        pending.append(copy)
        return copy

    loads = [pltpu.make_async_copy(m_hbm, m_ref, load.at[0]), pltpu.make_async_copy(cw_hbm, cw, load.at[1])]
    for copy in loads:
        copy.start()
    barrier = pltpu.get_barrier_semaphore()
    partners = [{"gz": other}] + [{"gy": lax.rem(cy + d, ny)} for d in range(1, ny)]
    partners += [{"gx": lax.rem(cx + d, nx)} for d in range(1, nx)]
    for partner in partners:
        pl.semaphore_signal(barrier, inc=1, device_id=partner, device_id_type=pl.DeviceIdType.MESH)
    for copy in loads:
        copy.wait()
    for a in range(3):
        m = m_ref[a].reshape(cells, width)
        ezt[0, pl.ds(0, cells), :] = m
        top = ezt[0, pl.ds(lz - 1, lx * ly, stride=lz), :]
        bottom = ezt[0, pl.ds(0, lx * ly, stride=lz), :]
        z_out[a] = jnp.where(cz == 0, top, bottom)
    pl.semaphore_wait(barrier, len(partners))

    arrivals = [
        remote(m_ref.at[:, pl.ds(lx - 1, 1)], x_before, face_send.at[0], face_recv.at[0], {"gx": lax.rem(cx + 1, nx)}),
        remote(m_ref.at[:, pl.ds(0, 1)], x_after, face_send.at[1], face_recv.at[1], {"gx": lax.rem(cx + nx - 1, nx)}),
        remote(m_ref.at[:, :, pl.ds(plane - 8, 8)], y_before, face_send.at[2], face_recv.at[2],
               {"gy": lax.rem(cy + 1, ny)}),
        remote(m_ref.at[:, :, pl.ds(0, 8)], y_after, face_send.at[3], face_recv.at[3],
               {"gy": lax.rem(cy + ny - 1, ny)}),
        remote(z_out, z_face, face_send.at[4], face_recv.at[4], {"gz": other}),
    ]
    for x in range(lx):
        turned = cw[x].T * scale
        for z in range(lz):
            column = jnp.broadcast_to(turned[:, z:z + 1], (ly, LANES))
            wide[pl.ds(x * plane + z, ly, stride=lz), :] = column
    weight = wide[:, :TEST]
    for a in range(3):
        m = m_ref[a].reshape(cells, width)
        mt[a, pl.ds(0, width), :] = m.T
        mt[a, pl.ds(width, 8), :] = jnp.zeros((8, cells), jnp.float32)
        high, low = split(m[:, :TEST] * weight)
        rhs[pl.ds(a * cells, cells), :] = jnp.concatenate([high, low], axis=1)
        rhs[pl.ds((3 + a) * cells, cells), :] = jnp.concatenate([high, jnp.zeros_like(low)], axis=1)
    spare = hbuf.shape[1] - pairs
    for a in range(3):
        hbuf[a, pl.ds(pairs, spare), :] = jnp.zeros((spare, cells), jnp.float32)
    for copy in arrivals:
        copy.wait_recv()
    transposed_gradients(lx, ly, lz, cz, m_ref, (x_before, x_after, y_before, y_after, z_face), gt, ext, eyt, ezt)
    pair_products(width, mt, gt, hbuf)

    orders = [list(range(bits)), list(reversed(range(bits)))]
    masks = [[sum((r >> (bits - 1 - k) & 1) << b for k, b in enumerate(orders[h])) for r in range(ny)] for h in range(2)]

    def products(c, h, level, into):
        rows_from, count = parts[c]
        for r in range(ny):
            @pl.loop(0, hx)
            def _(t):
                slot = ((h * hx + t) * ny + position(masks[h][r])) * nz + level
                start = owner[slot] * block + rows_from
                at = pl.ds(pl.multiple_of((r * hx + t) * 2 * count, 16), 2 * count)
                for a in range(3):
                    both = [hbuf[a, pl.ds(start, count), :], hbuf[a, pl.ds(start + half, count), :]]
                    high, low = split(jnp.concatenate(both, axis=0))
                    lhs[at, pl.ds(a * cells, cells)] = high
                    lhs[at, pl.ds((3 + a) * cells, cells)] = low

        result = jnp.dot(lhs[pl.ds(0, ny * hx * 2 * count), :], rhs[...], preferred_element_type=jnp.float32)
        result = (result + pltpu.roll(result, TEST, 1)).reshape(ny, hx, 2, count, LANES)
        first = lax.broadcasted_iota(jnp.int32, (ny, hx, count, LANES), 3) < TEST
        into[h, :, :, pl.ds(rows_from, count), :] = jnp.where(first, result[:, :, 0], result[:, :, 1])

    first_hop, hops, lines = {}, {}, {}

    def send(c, h, k):
        n = ny >> (k + 1)
        rows = pl.ds(*parts[c])
        hops[c, h, k] = remote(acc.at[h, pl.ds(n, n), :, rows], from_gy.at[h, pl.ds(n, n), :, rows],
                               gy_send.at[c, h, k], gy_recv.at[c, h, k], {"gy": position(1 << orders[h][k])})

    def across_cores(c):
        rows = pl.ds(*parts[c])
        for h in range(2):
            products(c, h, other, part)
            first_hop[c, h] = remote(part.at[h, :, :, rows], from_core.at[h, :, :, rows], core_send.at[c, h],
                                     core_recv.at[c, h], {"gz": other})

    def chip_sums(c):
        rows = pl.ds(*parts[c])
        for h in range(2):
            products(c, h, cz, acc)
            first_hop[c, h].wait_recv()
            acc[h, :, :, rows, :] = acc[h, :, :, rows, :] + from_core[h, :, :, rows, :]
            send(c, h, 0)

    def across_gy(c, k):
        n = ny >> (k + 1)
        rows = pl.ds(*parts[c])
        for h in range(2):
            hops[c, h, k].wait_recv()
            acc[h, pl.ds(0, n), :, rows, :] = acc[h, pl.ds(0, n), :, rows, :] + from_gy[h, pl.ds(n, n), :, rows, :]
            if k < bits - 1:
                send(c, h, k + 1)
        if k == bits - 1:
            for d in range(1, nx):
                to = lax.rem(cx + d, nx)
                lines[c, d] = remote(acc.at[to // hx, 0, lax.rem(to, hx), rows], from_gx.at[d - 1, rows],
                                     gx_send.at[c, d - 1], gx_recv.at[c, d - 1], {"gx": to})

    stages = [across_cores, chip_sums] + [functools.partial(across_gy, k=k) for k in range(bits)]
    for wave in range(len(parts) + len(stages) - 1):
        for k, stage in enumerate(stages):
            if 0 <= wave - k < len(parts):
                stage(wave - k)
    sums = []
    for c, (rows_from, count) in enumerate(parts):
        rows = pl.ds(rows_from, count)
        total = acc[cx // hx, 0, lax.rem(cx, hx), rows, :]
        for d in range(1, nx):
            lines[c, d].wait_recv()
            total = total + from_gx[d - 1, rows, :]
        sums.append(total)
    turned = jnp.concatenate(sums, axis=0).T
    out[...] = jnp.concatenate([turned[:TEST, :half], turned[TEST:, :block - half]], axis=1)
    for copy in pending:
        copy.wait_send()


def shards(modes, cell_weight, pair_owner):
    _, lx, ly, lz, width = modes.shape
    nx, ny, nz = (lax.axis_size(name) for name in ("gx", "gy", "gz"))
    slots = nx * ny * nz
    cells, plane = lx * ly * lz, ly * lz
    pairs = width * (width + 1) // 2
    block = (pairs + slots - 1) // slots
    half = (block + 1) // 2
    rows = (half + 7) // 8 * 8
    hx = nx // 2
    scale = 1.0 / math.sqrt(3.0 * cells * slots)
    table_rows = (slots * block + half + rows + 7) // 8 * 8
    stages = len(bounds(rows))
    longest = max(count for _, count in bounds(rows))
    bits = ny.bit_length() - 1
    vmem = pl.BlockSpec(memory_space=pltpu.VMEM)
    hbm = pl.BlockSpec(memory_space=pltpu.HBM)
    dma = pltpu.SemaphoreType.DMA

    def buffer(*shape):
        return pltpu.VMEM(shape, jnp.float32)

    return pl.pallas_call(
        functools.partial(convective_kernel, (nx, ny, nz), (lx, ly, lz), block, scale),
        out_shape=jax.ShapeDtypeStruct((TEST, block), jnp.float32),
        in_specs=[pl.BlockSpec(memory_space=pltpu.SMEM), hbm, hbm],
        out_specs=vmem,
        scratch_shapes=[
            buffer(3, lx, plane, width), buffer(lx, lz, ly), dma((2,)),
            buffer(3, 1, plane, width), buffer(3, 1, plane, width),
            buffer(3, lx, 8, width), buffer(3, lx, 8, width),
            buffer(3, lx * ly, width), buffer(3, lx * ly, width),
            buffer(3, width + 8, cells), buffer(9, width + 8, cells),
            buffer(3, table_rows, cells), pltpu.VMEM((ny * hx * 2 * longest, 6 * cells), jnp.bfloat16),
            pltpu.VMEM((6 * cells, LANES), jnp.bfloat16), buffer(cells, LANES),
            buffer(cells + 2 * plane, width), buffer(lx, plane + 2 * lz, width), buffer(2, cells + 16, width),
            buffer(2, ny, hx, rows, LANES), buffer(2, ny, hx, rows, LANES),
            buffer(2, ny, hx, rows, LANES), buffer(2, ny, hx, rows, LANES),
            buffer(nx - 1, rows, LANES),
            dma((5,)), dma((5,)),
        ] + [dma((stages, 2))] * 2 + [dma((stages, 2, bits))] * 2 + [dma((stages, nx - 1))] * 2,
        compiler_params=pltpu.CompilerParams(
            collective_id=0, has_side_effects=True, vmem_limit_bytes=62 * 1024 * 1024
        ),
    )(pair_owner, modes.reshape(3, lx, plane, width), cell_weight.transpose(0, 2, 1))


def solution(mesh):
    placed = (P("groups", "gx", "gy", "gz", None), P("gx", "gy", "gz"), P())
    return jax.shard_map(
        shards,
        mesh=mesh,
        in_specs=placed,
        out_specs=P("groups", ("gx", "gy", "gz")),
        check_vma=False,
    )
```

```python
import functools
import math
import jax
import jax.numpy as jnp
from jax import lax
from jax.experimental import pallas as pl
from jax.experimental.pallas import tpu as pltpu
from jax.sharding import PartitionSpec as P

TEST = 64
LANES = 128
STAGES = 2
UNROLL = 4


def bounds(rows):
    tiles = rows // 8
    stages = min(STAGES, tiles)
    cuts = [8 * (tiles * c // stages) for c in range(stages + 1)]
    return [(a, b - a) for a, b in zip(cuts, cuts[1:])]


def transposed_gradients(lx, ly, lz, level, m_ref, faces, gt, ext, eyt, ezt):
    cells, plane, width = lx * ly * lz, ly * lz, m_ref.shape[-1]
    x_before, x_after, y_before, y_after, z_face = faces
    for a in range(3):
        m = m_ref[a].reshape(cells, width)
        ext[pl.ds(0, plane), :] = x_before[a, 0]
        ext[pl.ds(plane, cells), :] = m
        ext[pl.ds(plane + cells, plane), :] = x_after[a, 0]
        step = (ext[pl.ds(2 * plane, cells), :] - ext[pl.ds(0, cells), :]) * 0.5
        gt[3 * a, pl.ds(0, width), :] = step.T
        for x in range(lx):
            eyt[x, pl.ds(0, lz), :] = y_before[a, x, pl.ds(8 - lz, lz), :]
            eyt[x, pl.ds(lz, plane), :] = m_ref[a, x]
            eyt[x, pl.ds(lz + plane, lz), :] = y_after[a, x, pl.ds(0, lz), :]
        step = (eyt[:, pl.ds(2 * lz, plane), :] - eyt[:, pl.ds(0, plane), :]) * 0.5
        gt[3 * a + 1, pl.ds(0, width), :] = step.reshape(cells, width).T
        ezt[0, pl.ds(8, cells), :] = m
        ezt[1, pl.ds(0, cells), :] = ezt[0, pl.ds(9, cells), :]
        ezt[0, pl.ds(0, cells), :] = ezt[0, pl.ds(7, cells), :]
        ezt[0, pl.ds(0, lx * ly, stride=lz), :] = jnp.where(level == 1, z_face[a], 0.0)
        ezt[1, pl.ds(lz - 1, lx * ly, stride=lz), :] = jnp.where(level == 0, z_face[a], 0.0)
        step = (ezt[1, pl.ds(0, cells), :] - ezt[0, pl.ds(0, cells), :]) * 0.5
        gt[3 * a + 2, pl.ds(0, width), :] = step.T
        for b in range(3):
            gt[3 * a + b, pl.ds(width, 8), :] = jnp.zeros((8, cells), jnp.float32)


def pair_products(width, mt, gt, hbuf):
    for group in range(width // 8):
        tiles = width // 8 - group

        @pl.loop(0, 8 // UNROLL)
        def _(step):
            for ahead in range(UNROLL):
                j = group * 8 + step * UNROLL + ahead
                start = j * width - (j * (j - 1)) // 2
                mj = [mt[b, pl.ds(j, 1), :] for b in range(3)]
                gj = [gt[c, pl.ds(j, 1), :] for c in range(9)]
                for t in range(tiles):
                    mk = [mt[b, pl.ds(j + 8 * t, 8), :] for b in range(3)]
                    for a in range(3):
                        terms = [
                            mj[b] * gt[3 * a + b, pl.ds(j + 8 * t, 8), :] + gj[3 * a + b] * mk[b]
                            for b in range(3)
                        ]
                        hbuf[a, pl.ds(start + 8 * t, 8), :] = terms[0] + terms[1] + terms[2]


def split(value):
    high = value.astype(jnp.bfloat16)
    return high, (value - high.astype(jnp.float32)).astype(jnp.bfloat16)


def bit_of(value, bit):
    return lax.rem(value // (1 << bit), 2)


def convective_kernel(mesh_shape, local_shape, block, scale, owner, m_hbm, cw_hbm, out, m_ref, cw, load,
                      x_before, x_after, y_before, y_after, z_face, z_out, mt, gt, hbuf, lhs, rhs, wide, ext, eyt, ezt,
                      part, acc, from_core, from_gy, from_gx, face_send, face_recv,
                      core_send, core_recv, gy_send, gy_recv, gx_send, gx_recv):
    nx, ny, nz = mesh_shape
    lx, ly, lz = local_shape
    cells, plane, width = lx * ly * lz, ly * lz, m_ref.shape[-1]
    pairs = width * (width + 1) // 2
    half = (block + 1) // 2
    hx = nx // 2
    parts = bounds(acc.shape[3])
    cx, cy, cz = (lax.axis_index(name) for name in ("gx", "gy", "gz"))
    other = 1 - cz
    bits = ny.bit_length() - 1
    mine = [bit_of(cy, b) for b in range(bits)]

    def position(mask):
        return sum((1 - mine[b] if mask >> b & 1 else mine[b]) * (1 << b) for b in range(bits))

    pending = []

    def remote(src, dst, send, recv, device):
        copy = pltpu.make_async_remote_copy(
            src_ref=src, dst_ref=dst, send_sem=send, recv_sem=recv, device_id=device,
            device_id_type=pl.DeviceIdType.MESH,
        )
        copy.start()
        pending.append(copy)
        return copy

    loads = [pltpu.make_async_copy(m_hbm, m_ref, load.at[0]), pltpu.make_async_copy(cw_hbm, cw, load.at[1])]
    for copy in loads:
        copy.start()
    barrier = pltpu.get_barrier_semaphore()
    partners = [{"gz": other}] + [{"gy": lax.rem(cy + d, ny)} for d in range(1, ny)]
    partners += [{"gx": lax.rem(cx + d, nx)} for d in range(1, nx)]
    for partner in partners:
        pl.semaphore_signal(barrier, inc=1, device_id=partner, device_id_type=pl.DeviceIdType.MESH)
    for copy in loads:
        copy.wait()
    for a in range(3):
        m = m_ref[a].reshape(cells, width)
        ezt[0, pl.ds(0, cells), :] = m
        top = ezt[0, pl.ds(lz - 1, lx * ly, stride=lz), :]
        bottom = ezt[0, pl.ds(0, lx * ly, stride=lz), :]
        z_out[a] = jnp.where(cz == 0, top, bottom)
    pl.semaphore_wait(barrier, len(partners))

    arrivals = [
        remote(m_ref.at[:, pl.ds(lx - 1, 1)], x_before, face_send.at[0], face_recv.at[0], {"gx": lax.rem(cx + 1, nx)}),
        remote(m_ref.at[:, pl.ds(0, 1)], x_after, face_send.at[1], face_recv.at[1], {"gx": lax.rem(cx + nx - 1, nx)}),
        remote(m_ref.at[:, :, pl.ds(plane - 8, 8)], y_before, face_send.at[2], face_recv.at[2],
               {"gy": lax.rem(cy + 1, ny)}),
        remote(m_ref.at[:, :, pl.ds(0, 8)], y_after, face_send.at[3], face_recv.at[3],
               {"gy": lax.rem(cy + ny - 1, ny)}),
        remote(z_out, z_face, face_send.at[4], face_recv.at[4], {"gz": other}),
    ]
    for x in range(lx):
        turned = cw[x].T * scale
        for z in range(lz):
            column = jnp.broadcast_to(turned[:, z:z + 1], (ly, LANES))
            wide[pl.ds(x * plane + z, ly, stride=lz), :] = column
    weight = wide[:, :TEST]
    for a in range(3):
        m = m_ref[a].reshape(cells, width)
        mt[a, pl.ds(0, width), :] = m.T
        mt[a, pl.ds(width, 8), :] = jnp.zeros((8, cells), jnp.float32)
        high, low = split(m[:, :TEST] * weight)
        rhs[pl.ds(a * cells, cells), :] = jnp.concatenate([high, low], axis=1)
        rhs[pl.ds((3 + a) * cells, cells), :] = jnp.concatenate([high, jnp.zeros_like(low)], axis=1)
    spare = hbuf.shape[1] - pairs
    for a in range(3):
        hbuf[a, pl.ds(pairs, spare), :] = jnp.zeros((spare, cells), jnp.float32)
    for copy in arrivals:
        copy.wait_recv()
    transposed_gradients(lx, ly, lz, cz, m_ref, (x_before, x_after, y_before, y_after, z_face), gt, ext, eyt, ezt)
    pair_products(width, mt, gt, hbuf)

    orders = [list(range(bits)), list(reversed(range(bits)))]
    masks = [[sum((r >> (bits - 1 - k) & 1) << b for k, b in enumerate(orders[h])) for r in range(ny)] for h in range(2)]

    def products(c, h, level, into):
        rows_from, count = parts[c]
        for r in range(ny):
            @pl.loop(0, hx)
            def _(t):
                slot = ((h * hx + t) * ny + position(masks[h][r])) * nz + level
                start = owner[slot] * block + rows_from
                at = pl.ds(pl.multiple_of((r * hx + t) * 2 * count, 16), 2 * count)
                for a in range(3):
                    both = [hbuf[a, pl.ds(start, count), :], hbuf[a, pl.ds(start + half, count), :]]
                    high, low = split(jnp.concatenate(both, axis=0))
                    lhs[at, pl.ds(a * cells, cells)] = high
                    lhs[at, pl.ds((3 + a) * cells, cells)] = low

        result = jnp.dot(lhs[pl.ds(0, ny * hx * 2 * count), :], rhs[...], preferred_element_type=jnp.float32)
        result = (result + pltpu.roll(result, TEST, 1)).reshape(ny, hx, 2, count, LANES)
        first = lax.broadcasted_iota(jnp.int32, (ny, hx, count, LANES), 3) < TEST
        into[h, :, :, pl.ds(rows_from, count), :] = jnp.where(first, result[:, :, 0], result[:, :, 1])

    first_hop, hops, lines = {}, {}, {}

    def send(c, h, k):
        n = ny >> (k + 1)
        rows = pl.ds(*parts[c])
        hops[c, h, k] = remote(acc.at[h, pl.ds(n, n), :, rows], from_gy.at[h, pl.ds(n, n), :, rows],
                               gy_send.at[c, h, k], gy_recv.at[c, h, k], {"gy": position(1 << orders[h][k])})

    def across_cores(c):
        rows = pl.ds(*parts[c])
        for h in range(2):
            products(c, h, other, part)
            first_hop[c, h] = remote(part.at[h, :, :, rows], from_core.at[h, :, :, rows], core_send.at[c, h],
                                     core_recv.at[c, h], {"gz": other})

    def chip_sums(c):
        rows = pl.ds(*parts[c])
        for h in range(2):
            products(c, h, cz, acc)
            first_hop[c, h].wait_recv()
            acc[h, :, :, rows, :] = acc[h, :, :, rows, :] + from_core[h, :, :, rows, :]
            send(c, h, 0)

    def across_gy(c, k):
        n = ny >> (k + 1)
        rows = pl.ds(*parts[c])
        for h in range(2):
            hops[c, h, k].wait_recv()
            acc[h, pl.ds(0, n), :, rows, :] = acc[h, pl.ds(0, n), :, rows, :] + from_gy[h, pl.ds(n, n), :, rows, :]
            if k < bits - 1:
                send(c, h, k + 1)
        if k == bits - 1:
            for d in range(1, nx):
                to = lax.rem(cx + d, nx)
                lines[c, d] = remote(acc.at[to // hx, 0, lax.rem(to, hx), rows], from_gx.at[d - 1, rows],
                                     gx_send.at[c, d - 1], gx_recv.at[c, d - 1], {"gx": to})

    def chip(c):
        across_cores(c)
        chip_sums(c)

    stages = [chip] + [functools.partial(across_gy, k=k) for k in range(bits)]
    for wave in range(len(parts) + len(stages) - 1):
        for k, stage in enumerate(stages):
            if 0 <= wave - k < len(parts):
                stage(wave - k)
    sums = []
    for c, (rows_from, count) in enumerate(parts):
        rows = pl.ds(rows_from, count)
        total = acc[cx // hx, 0, lax.rem(cx, hx), rows, :]
        for d in range(1, nx):
            lines[c, d].wait_recv()
            total = total + from_gx[d - 1, rows, :]
        sums.append(total)
    turned = jnp.concatenate(sums, axis=0).T
    out[...] = jnp.concatenate([turned[:TEST, :half], turned[TEST:, :block - half]], axis=1)
    for copy in pending:
        copy.wait_send()


def shards(modes, cell_weight, pair_owner):
    _, lx, ly, lz, width = modes.shape
    nx, ny, nz = (lax.axis_size(name) for name in ("gx", "gy", "gz"))
    slots = nx * ny * nz
    cells, plane = lx * ly * lz, ly * lz
    pairs = width * (width + 1) // 2
    block = (pairs + slots - 1) // slots
    half = (block + 1) // 2
    rows = (half + 7) // 8 * 8
    hx = nx // 2
    scale = 1.0 / math.sqrt(3.0 * cells * slots)
    table_rows = (slots * block + half + rows + 7) // 8 * 8
    stages = len(bounds(rows))
    longest = max(count for _, count in bounds(rows))
    bits = ny.bit_length() - 1
    vmem = pl.BlockSpec(memory_space=pltpu.VMEM)
    hbm = pl.BlockSpec(memory_space=pltpu.HBM)
    dma = pltpu.SemaphoreType.DMA

    def buffer(*shape):
        return pltpu.VMEM(shape, jnp.float32)

    return pl.pallas_call(
        functools.partial(convective_kernel, (nx, ny, nz), (lx, ly, lz), block, scale),
        out_shape=jax.ShapeDtypeStruct((TEST, block), jnp.float32),
        in_specs=[pl.BlockSpec(memory_space=pltpu.SMEM), hbm, hbm],
        out_specs=vmem,
        scratch_shapes=[
            buffer(3, lx, plane, width), buffer(lx, lz, ly), dma((2,)),
            buffer(3, 1, plane, width), buffer(3, 1, plane, width),
            buffer(3, lx, 8, width), buffer(3, lx, 8, width),
            buffer(3, lx * ly, width), buffer(3, lx * ly, width),
            buffer(3, width + 8, cells), buffer(9, width + 8, cells),
            buffer(3, table_rows, cells), pltpu.VMEM((ny * hx * 2 * longest, 6 * cells), jnp.bfloat16),
            pltpu.VMEM((6 * cells, LANES), jnp.bfloat16), buffer(cells, LANES),
            buffer(cells + 2 * plane, width), buffer(lx, plane + 2 * lz, width), buffer(2, cells + 16, width),
            buffer(2, ny, hx, rows, LANES), buffer(2, ny, hx, rows, LANES),
            buffer(2, ny, hx, rows, LANES), buffer(2, ny, hx, rows, LANES),
            buffer(nx - 1, rows, LANES),
            dma((5,)), dma((5,)),
        ] + [dma((stages, 2))] * 2 + [dma((stages, 2, bits))] * 2 + [dma((stages, nx - 1))] * 2,
        compiler_params=pltpu.CompilerParams(
            collective_id=0, has_side_effects=True, vmem_limit_bytes=62 * 1024 * 1024
        ),
    )(pair_owner, modes.reshape(3, lx, plane, width), cell_weight.transpose(0, 2, 1))


def solution(mesh):
    placed = (P("groups", "gx", "gy", "gz", None), P("gx", "gy", "gz"), P())
    return jax.shard_map(
        shards,
        mesh=mesh,
        in_specs=placed,
        out_specs=P("groups", ("gx", "gy", "gz")),
        check_vma=False,
    )
```

```python
import functools
import math
import jax
import jax.numpy as jnp
from jax import lax
from jax.experimental import pallas as pl
from jax.experimental.pallas import tpu as pltpu
from jax.sharding import PartitionSpec as P

TEST = 64
LANES = 128
STAGES = 2
UNROLL = 2
CHUNK = 688


def bounds(rows):
    tiles = rows // 8
    stages = min(STAGES, tiles)
    cuts = [8 * (tiles * c // stages) for c in range(stages + 1)]
    return [(a, b - a) for a, b in zip(cuts, cuts[1:])]


def transposed_gradients(lx, ly, lz, level, m_ref, faces, gt, ext, eyt, ezt):
    cells, plane, width = lx * ly * lz, ly * lz, m_ref.shape[-1]
    x_before, x_after, y_before, y_after, z_face = faces
    for a in range(3):
        m = m_ref[a].reshape(cells, width)
        ext[pl.ds(0, plane), :] = x_before[a, 0]
        ext[pl.ds(plane, cells), :] = m
        ext[pl.ds(plane + cells, plane), :] = x_after[a, 0]
        step = (ext[pl.ds(2 * plane, cells), :] - ext[pl.ds(0, cells), :]) * 0.5
        gt[3 * a, pl.ds(0, width), :] = step.T
        for x in range(lx):
            eyt[x, pl.ds(0, lz), :] = y_before[a, x, pl.ds(8 - lz, lz), :]
            eyt[x, pl.ds(lz, plane), :] = m_ref[a, x]
            eyt[x, pl.ds(lz + plane, lz), :] = y_after[a, x, pl.ds(0, lz), :]
        step = (eyt[:, pl.ds(2 * lz, plane), :] - eyt[:, pl.ds(0, plane), :]) * 0.5
        gt[3 * a + 1, pl.ds(0, width), :] = step.reshape(cells, width).T
        ezt[0, pl.ds(8, cells), :] = m
        ezt[1, pl.ds(0, cells), :] = ezt[0, pl.ds(9, cells), :]
        ezt[0, pl.ds(0, cells), :] = ezt[0, pl.ds(7, cells), :]
        ezt[0, pl.ds(0, lx * ly, stride=lz), :] = jnp.where(level == 1, z_face[a], 0.0)
        ezt[1, pl.ds(lz - 1, lx * ly, stride=lz), :] = jnp.where(level == 0, z_face[a], 0.0)
        step = (ezt[1, pl.ds(0, cells), :] - ezt[0, pl.ds(0, cells), :]) * 0.5
        gt[3 * a + 2, pl.ds(0, width), :] = step.T
        for b in range(3):
            gt[3 * a + b, pl.ds(width, 8), :] = jnp.zeros((8, cells), jnp.float32)


def pair_products(width, mt, gt, hbuf):
    for group in range(width // 8):
        tiles = width // 8 - group

        @pl.loop(0, 8 // UNROLL)
        def _(step):
            for ahead in range(UNROLL):
                j = group * 8 + step * UNROLL + ahead
                start = j * width - (j * (j - 1)) // 2
                mj = [mt[b, pl.ds(j, 1), :] for b in range(3)]
                gj = [gt[c, pl.ds(j, 1), :] for c in range(9)]
                for t in range(tiles):
                    mk = [mt[b, pl.ds(j + 8 * t, 8), :] for b in range(3)]
                    for a in range(3):
                        terms = [
                            mj[b] * gt[3 * a + b, pl.ds(j + 8 * t, 8), :] + gj[3 * a + b] * mk[b]
                            for b in range(3)
                        ]
                        hbuf[a, pl.ds(start + 8 * t, 8), :] = terms[0] + terms[1] + terms[2]


def split(value):
    high = value.astype(jnp.bfloat16)
    return high, (value - high.astype(jnp.float32)).astype(jnp.bfloat16)


def bit_of(value, bit):
    return lax.rem(value // (1 << bit), 2)


def convective_kernel(mesh_shape, local_shape, block, scale, owner, m_hbm, cw_hbm, out, m_ref, cw, load,
                      x_before, x_after, y_before, y_after, z_face, z_out, mt, gt, hbuf, sbuf, rhs, wide, ext, eyt, ezt,
                      part, acc, from_core, from_gy, from_gx, face_send, face_recv,
                      core_send, core_recv, gy_send, gy_recv, gx_send, gx_recv):
    nx, ny, nz = mesh_shape
    lx, ly, lz = local_shape
    cells, plane, width = lx * ly * lz, ly * lz, m_ref.shape[-1]
    pairs = width * (width + 1) // 2
    half = (block + 1) // 2
    hx = nx // 2
    parts = bounds(acc.shape[3])
    cx, cy, cz = (lax.axis_index(name) for name in ("gx", "gy", "gz"))
    other = 1 - cz
    bits = ny.bit_length() - 1
    mine = [bit_of(cy, b) for b in range(bits)]

    def position(mask):
        return sum((1 - mine[b] if mask >> b & 1 else mine[b]) * (1 << b) for b in range(bits))

    pending = []

    def remote(src, dst, send, recv, device):
        copy = pltpu.make_async_remote_copy(
            src_ref=src, dst_ref=dst, send_sem=send, recv_sem=recv, device_id=device,
            device_id_type=pl.DeviceIdType.MESH,
        )
        copy.start()
        pending.append(copy)
        return copy

    loads = [pltpu.make_async_copy(m_hbm, m_ref, load.at[0]), pltpu.make_async_copy(cw_hbm, cw, load.at[1])]
    for copy in loads:
        copy.start()
    barrier = pltpu.get_barrier_semaphore()
    partners = [{"gz": other}] + [{"gy": lax.rem(cy + d, ny)} for d in range(1, ny)]
    partners += [{"gx": lax.rem(cx + d, nx)} for d in range(1, nx)]
    for partner in partners:
        pl.semaphore_signal(barrier, inc=1, device_id=partner, device_id_type=pl.DeviceIdType.MESH)
    for copy in loads:
        copy.wait()
    for a in range(3):
        m = m_ref[a].reshape(cells, width)
        ezt[0, pl.ds(0, cells), :] = m
        top = ezt[0, pl.ds(lz - 1, lx * ly, stride=lz), :]
        bottom = ezt[0, pl.ds(0, lx * ly, stride=lz), :]
        z_out[a] = jnp.where(cz == 0, top, bottom)
    pl.semaphore_wait(barrier, len(partners))

    arrivals = [
        remote(m_ref.at[:, pl.ds(lx - 1, 1)], x_before, face_send.at[0], face_recv.at[0], {"gx": lax.rem(cx + 1, nx)}),
        remote(m_ref.at[:, pl.ds(0, 1)], x_after, face_send.at[1], face_recv.at[1], {"gx": lax.rem(cx + nx - 1, nx)}),
        remote(m_ref.at[:, :, pl.ds(plane - 8, 8)], y_before, face_send.at[2], face_recv.at[2],
               {"gy": lax.rem(cy + 1, ny)}),
        remote(m_ref.at[:, :, pl.ds(0, 8)], y_after, face_send.at[3], face_recv.at[3],
               {"gy": lax.rem(cy + ny - 1, ny)}),
        remote(z_out, z_face, face_send.at[4], face_recv.at[4], {"gz": other}),
    ]
    for x in range(lx):
        turned = cw[x].T * scale
        for z in range(lz):
            column = jnp.broadcast_to(turned[:, z:z + 1], (ly, LANES))
            wide[pl.ds(x * plane + z, ly, stride=lz), :] = column
    weight = wide[:, :TEST]
    for a in range(3):
        m = m_ref[a].reshape(cells, width)
        mt[a, pl.ds(0, width), :] = m.T
        mt[a, pl.ds(width, 8), :] = jnp.zeros((8, cells), jnp.float32)
        high, low = split(m[:, :TEST] * weight)
        rhs[pl.ds(a * cells, cells), :] = jnp.concatenate([high, low], axis=1)
        rhs[pl.ds((3 + a) * cells, cells), :] = jnp.concatenate([high, jnp.zeros_like(low)], axis=1)
    spare = sbuf.shape[0] - pairs
    sbuf[pl.ds(pairs, spare), :] = jnp.zeros((spare, LANES), jnp.float32)
    for copy in arrivals:
        copy.wait_recv()
    transposed_gradients(lx, ly, lz, cz, m_ref, (x_before, x_after, y_before, y_after, z_face), gt, ext, eyt, ezt)
    pair_products(width, mt, gt, hbuf)

    @pl.loop(0, pairs // CHUNK)
    def _(c):
        here = pl.ds(pl.multiple_of(c * CHUNK, 16), CHUNK)
        pieces = [split(hbuf[a, here, :]) for a in range(3)]
        left = jnp.concatenate([high for high, _ in pieces] + [low for _, low in pieces], axis=1)
        both = jnp.dot(left, rhs[...], preferred_element_type=jnp.float32)
        sbuf[here, :] = both + pltpu.roll(both, TEST, 1)

    orders = [list(range(bits)), list(reversed(range(bits)))]
    masks = [[sum((r >> (bits - 1 - k) & 1) << b for k, b in enumerate(orders[h])) for r in range(ny)] for h in range(2)]

    def products(c, h, level, into):
        rows_from, count = parts[c]
        first = lax.broadcasted_iota(jnp.int32, (count, LANES), 1) < TEST
        for r in range(ny):
            @pl.loop(0, hx)
            def _(t):
                slot = ((h * hx + t) * ny + position(masks[h][r])) * nz + level
                start = owner[slot] * block + rows_from
                low, high = sbuf[pl.ds(start, count), :], sbuf[pl.ds(start + half, count), :]
                into[h, r, t, pl.ds(rows_from, count), :] = jnp.where(first, low, high)

    first_hop, hops, lines = {}, {}, {}

    def send(c, h, k):
        n = ny >> (k + 1)
        rows = pl.ds(*parts[c])
        hops[c, h, k] = remote(acc.at[h, pl.ds(n, n), :, rows], from_gy.at[h, pl.ds(n, n), :, rows],
                               gy_send.at[c, h, k], gy_recv.at[c, h, k], {"gy": position(1 << orders[h][k])})

    def across_cores(c):
        rows = pl.ds(*parts[c])
        for h in range(2):
            products(c, h, other, part)
            first_hop[c, h] = remote(part.at[h, :, :, rows], from_core.at[h, :, :, rows], core_send.at[c, h],
                                     core_recv.at[c, h], {"gz": other})

    def chip_sums(c):
        rows = pl.ds(*parts[c])
        for h in range(2):
            products(c, h, cz, acc)
            first_hop[c, h].wait_recv()
            acc[h, :, :, rows, :] = acc[h, :, :, rows, :] + from_core[h, :, :, rows, :]
            send(c, h, 0)

    def across_gy(c, k):
        n = ny >> (k + 1)
        rows = pl.ds(*parts[c])
        for h in range(2):
            hops[c, h, k].wait_recv()
            acc[h, pl.ds(0, n), :, rows, :] = acc[h, pl.ds(0, n), :, rows, :] + from_gy[h, pl.ds(n, n), :, rows, :]
            if k < bits - 1:
                send(c, h, k + 1)
        if k == bits - 1:
            for d in range(1, nx):
                to = lax.rem(cx + d, nx)
                lines[c, d] = remote(acc.at[to // hx, 0, lax.rem(to, hx), rows], from_gx.at[d - 1, rows],
                                     gx_send.at[c, d - 1], gx_recv.at[c, d - 1], {"gx": to})

    def chip(c):
        across_cores(c)
        chip_sums(c)

    stages = [chip] + [functools.partial(across_gy, k=k) for k in range(bits)]
    for wave in range(len(parts) + len(stages) - 1):
        for k, stage in enumerate(stages):
            if 0 <= wave - k < len(parts):
                stage(wave - k)
    sums = []
    for c, (rows_from, count) in enumerate(parts):
        rows = pl.ds(rows_from, count)
        total = acc[cx // hx, 0, lax.rem(cx, hx), rows, :]
        for d in range(1, nx):
            lines[c, d].wait_recv()
            total = total + from_gx[d - 1, rows, :]
        sums.append(total)
    turned = jnp.concatenate(sums, axis=0).T
    out[...] = jnp.concatenate([turned[:TEST, :half], turned[TEST:, :block - half]], axis=1)
    for copy in pending:
        copy.wait_send()


def shards(modes, cell_weight, pair_owner):
    _, lx, ly, lz, width = modes.shape
    nx, ny, nz = (lax.axis_size(name) for name in ("gx", "gy", "gz"))
    slots = nx * ny * nz
    cells, plane = lx * ly * lz, ly * lz
    pairs = width * (width + 1) // 2
    block = (pairs + slots - 1) // slots
    half = (block + 1) // 2
    rows = (half + 7) // 8 * 8
    hx = nx // 2
    scale = 1.0 / math.sqrt(3.0 * cells * slots)
    table_rows = (slots * block + half + rows + 7) // 8 * 8
    stages = len(bounds(rows))
    bits = ny.bit_length() - 1
    vmem = pl.BlockSpec(memory_space=pltpu.VMEM)
    hbm = pl.BlockSpec(memory_space=pltpu.HBM)
    dma = pltpu.SemaphoreType.DMA

    def buffer(*shape):
        return pltpu.VMEM(shape, jnp.float32)

    return pl.pallas_call(
        functools.partial(convective_kernel, (nx, ny, nz), (lx, ly, lz), block, scale),
        out_shape=jax.ShapeDtypeStruct((TEST, block), jnp.float32),
        in_specs=[pl.BlockSpec(memory_space=pltpu.SMEM), hbm, hbm],
        out_specs=vmem,
        scratch_shapes=[
            buffer(3, lx, plane, width), buffer(lx, lz, ly), dma((2,)),
            buffer(3, 1, plane, width), buffer(3, 1, plane, width),
            buffer(3, lx, 8, width), buffer(3, lx, 8, width),
            buffer(3, lx * ly, width), buffer(3, lx * ly, width),
            buffer(3, width + 8, cells), buffer(9, width + 8, cells),
            buffer(3, pairs + 8, cells), buffer(table_rows, LANES),
            pltpu.VMEM((6 * cells, LANES), jnp.bfloat16), buffer(cells, LANES),
            buffer(cells + 2 * plane, width), buffer(lx, plane + 2 * lz, width), buffer(2, cells + 16, width),
            buffer(2, ny, hx, rows, LANES), buffer(2, ny, hx, rows, LANES),
            buffer(2, ny, hx, rows, LANES), buffer(2, ny, hx, rows, LANES),
            buffer(nx - 1, rows, LANES),
            dma((5,)), dma((5,)),
        ] + [dma((stages, 2))] * 2 + [dma((stages, 2, bits))] * 2 + [dma((stages, nx - 1))] * 2,
        compiler_params=pltpu.CompilerParams(
            collective_id=0, has_side_effects=True, vmem_limit_bytes=62 * 1024 * 1024
        ),
    )(pair_owner, modes.reshape(3, lx, plane, width), cell_weight.transpose(0, 2, 1))


def solution(mesh):
    placed = (P("groups", "gx", "gy", "gz", None), P("gx", "gy", "gz"), P())
    return jax.shard_map(
        shards,
        mesh=mesh,
        in_specs=placed,
        out_specs=P("groups", ("gx", "gy", "gz")),
        check_vma=False,
    )
```
